32 devices in a mesh: lat: 8 (over y, x, core), lon: 4 (over z).
Axes of the slice: x: 2, y: 2, z: 4, core: 2. Of those that a mesh axis runs over, the one named last changes fastest.
Arguments:
- vorticity: float32 [2, 1280, 2560], P(None, 'lat', 'lon'), may hold values from -46 to 46
- divergence: float32 [2, 1280, 2560], P(None, 'lat', 'lon'), may hold values from -46 to 46
- height: float32 [2, 1280, 2560], P(None, 'lat', 'lon'), may hold values from -46 to 46
- mean_geopot: float32 [2], replicated, may hold values from 0.5 to 8
Outputs:
- new_vorticity: float32 [2, 1280, 2560], P(None, 'lat', 'lon')
- new_divergence: float32 [2, 1280, 2560], P(None, 'lat', 'lon')
- new_height: float32 [2, 1280, 2560], P(None, 'lat', 'lon')
The draws below stay inside these ranges and needn't reach their ends.
All inputs are finite; a program needn't handle non-finite values.
Results may differ from the reference program's by a relative error of at most 0.0017.
Values sent between devices are 32-bit elements; how exact they have to be, the bound alone decides.
A program may use at most 448 MiB of HBM per device.

```python
import math
import jax
import jax.numpy as jnp
from jax import lax

NLON = 2560
NLAT = 1280
MMAX = 1280
LEV = 2


amplitude = 40.0


limit = 46.0


def banded_field(base_key, field_code):
    field_key = jax.random.fold_in(base_key, field_code)
    back_key, wave_key, phase_key = jax.random.split(field_key, 3)
    shape_all = (LEV, NLAT, NLON)
    background = jnp.clip(jax.random.normal(back_key, shape_all, jnp.float32), -6.0, 6.0)
    center = 1.0
    spread = 2.0
    row_index = jnp.arange(NLAT, dtype=jnp.float32)
    colatitude = (4.0 * row_index + 3.0) * jnp.pi / (4.0 * NLAT + 2.0)
    shortfall = 1.0 / (8.0 * NLAT * NLAT) - 1.0 / (8.0 * NLAT * NLAT * NLAT)
    one_minus = shortfall + 2.0 * (1.0 - shortfall) * jnp.sin(0.5 * colatitude) ** 2
    one_plus = shortfall + 2.0 * (1.0 - shortfall) * jnp.cos(0.5 * colatitude) ** 2
    sine_rows = jnp.sqrt(one_minus * one_plus)
    offsets = jax.random.randint(wave_key, (LEV, 4), 0, max(MMAX // 16, 1), dtype=jnp.int32)
    orders = MMAX // 4 + MMAX // 8 * jnp.arange(4, dtype=jnp.int32)[None, :] + offsets
    phases = jax.random.uniform(phase_key, (LEV, 4, 2), jnp.float32, -jnp.pi, jnp.pi)
    degree_top = MMAX - 0.5
    turning = orders.astype(jnp.float32) / degree_top
    cos_turn = jnp.sqrt(1.0 - turning * turning)
    widths = cos_turn * (2.0 * degree_top * degree_top * cos_turn / turning) ** (-1.0 / 3.0)
    north_rows = jnp.arange(NLAT, dtype=jnp.int32) < NLAT // 2
    points = jnp.arange(NLON, dtype=jnp.int32)
    total = background
    for band_index in range(4):
        order_now = orders[:, band_index]
        distance = (sine_rows[None, :] - turning[:, band_index, None]) / widths[:, band_index, None]
        profile = jnp.exp(-0.5 * ((distance - center) / spread) ** 2)
        row_phase = jnp.where(north_rows[None, :], phases[:, band_index, 0:1], phases[:, band_index, 1:2])
        angle_index = order_now[:, None] * points[None, :] % NLON
        wave_angle = angle_index.astype(jnp.float32) * (2.0 * jnp.pi / NLON)
        total = total + amplitude * profile[:, :, None] * jnp.cos(wave_angle[:, None, :] + row_phase[:, :, None])
    return jnp.clip(total, -limit, limit)


def draw_vorticity(key, part):
    return banded_field(key, 11)


def draw_divergence(key, part):
    return banded_field(key, 12)


def draw_height(key, part):
    return banded_field(key, 13)


def setup_inputs(seed: int = 0) -> dict:
    key_of = jax.random.split(jax.random.key(seed), 5)
    return {
        "vorticity": draw_vorticity(jax.random.fold_in(key_of[4], 71), 0),
        "divergence": draw_divergence(jax.random.fold_in(key_of[4], 71), 0),
        "height": draw_height(jax.random.fold_in(key_of[4], 71), 0),
        "mean_geopot": jnp.clip(jnp.exp(jax.random.uniform(key_of[3], (LEV,), jnp.float32, math.log(0.5), math.log(8.0))), 0.5, 8.0),
    }


cap_sine = 0.5
filter_width = 64.0
diffusion = 4.0
renorm_big = 2.0 ** 64
renorm_step = 64.0

def latitudes(row_index):
    colatitude = (4.0 * row_index + 3.0) * jnp.pi / (4.0 * NLAT + 2.0)
    shortfall = 1.0 / (8.0 * NLAT * NLAT) - 1.0 / (8.0 * NLAT * NLAT * NLAT)
    one_minus = shortfall + 2.0 * (1.0 - shortfall) * jnp.sin(0.5 * colatitude) ** 2
    one_plus = shortfall + 2.0 * (1.0 - shortfall) * jnp.cos(0.5 * colatitude) ** 2
    return (0.5 * (one_plus - one_minus), jnp.sqrt(one_minus * one_plus))

def sector_logs(float_type):
    sector_order = jnp.arange(1, MMAX, dtype=float_type)
    log_terms = jnp.log2((2.0 * sector_order + 1.0) / (2.0 * sector_order))
    return jnp.concatenate([jnp.zeros((1,), float_type), jnp.cumsum(log_terms)])

def advance(recurrence, excess_degree, wave_col, cosine, wave_limit):
    previous, current, exponent = recurrence
    degree = wave_col + excess_degree
    first_row = excess_degree == 0
    growth = jnp.sqrt((4.0 * degree * degree - 1.0) / jnp.maximum(excess_degree * (2.0 * wave_col + excess_degree), 1.0))
    backward = jnp.sqrt(jnp.maximum((excess_degree - 1.0) * (2.0 * wave_col + excess_degree - 1.0), 0.0) / jnp.maximum(4.0 * (degree - 1.0) ** 2 - 1.0, 1.0))
    following = growth * (cosine * current - backward * previous)
    too_large = jnp.abs(following) > renorm_big
    factor = jnp.where(too_large, 1.0 / renorm_big, 1.0)
    rescaled = (current * factor, following * factor, exponent + jnp.where(too_large, renorm_step, 0.0))
    new_state = jax.tree.map(lambda kept, changed: jnp.where(first_row, kept, changed), recurrence, rescaled)
    row_value = new_state[1] * jnp.exp2(new_state[2])
    row_value = jnp.where(excess_degree < wave_limit, row_value, 0.0)
    return (new_state, row_value)

def legendre_table(wavenumbers, cumlog_part, cosine, sine_theta):
    wave_col = wavenumbers[:, None]
    log_start = -0.5 + 0.5 * cumlog_part[:, None] + wave_col * jnp.log2(sine_theta)[None, :]
    exponent = jnp.floor(log_start)
    leading = jnp.exp2(log_start - exponent)
    recurrence = (jnp.zeros_like(leading), leading, exponent)
    wave_limit = MMAX - wave_col

    def advance_one(carry, excess_degree):
        return advance(carry, excess_degree, wave_col, cosine[None, :], wave_limit)
    _, row_values = lax.scan(advance_one, recurrence, jnp.arange(MMAX, dtype=wavenumbers.dtype))
    return jnp.transpose(row_values, (1, 0, 2))

def implicit(vort_part, div_part, height_part, degree, geopot):
    lap_ratio = degree * (degree + 1.0) / (MMAX * MMAX)
    coupling = jnp.sqrt(lap_ratio)
    damping = 1.0 / (1.0 + diffusion * lap_ratio * lap_ratio)
    div_new = (div_part + coupling * height_part) / (1.0 + geopot * coupling * coupling)
    height_new = height_part - geopot * coupling * div_new
    return (damping * vort_part, damping * div_new, damping * height_new)

def reference(vorticity, divergence, height, mean_geopot):
    float_type = vorticity.dtype
    fields = jnp.stack([vorticity, divergence, height])
    spectrum = jnp.fft.rfft(fields, axis=-1)[..., :MMAX] / NLON
    coeffs = jnp.stack([jnp.real(spectrum), jnp.imag(spectrum)]).astype(float_type)
    row_index = jnp.arange(NLAT, dtype=float_type)
    cosine, sine_theta = latitudes(row_index)
    weight = jnp.pi * sine_theta / (NLAT + 0.5)
    wavenumbers = jnp.arange(MMAX, dtype=float_type)
    excess = jnp.maximum(wavenumbers[None, :] - MMAX * sine_theta[:, None] / cap_sine, 0.0) / filter_width
    coeffs = coeffs * (weight[:, None] * jnp.exp(-0.5 * excess * excess))
    cumlog = sector_logs(float_type)
    block_count = MMAX // 16
    wave_blocks = jnp.moveaxis(coeffs.reshape(2, 3, LEV, NLAT, block_count, 16), 4, 0)

    def solve_block(pair_args):
        block_index, wave_block = pair_args
        wave_index = block_index * 16 + jnp.arange(16, dtype=jnp.int32)
        block_waves = wave_index.astype(float_type)
        legendre = legendre_table(block_waves, cumlog[wave_index], cosine, sine_theta)
        spectral = jnp.einsum('mkj,cfljm->cflmk', legendre, wave_block, precision=lax.Precision.HIGHEST)
        degree = block_waves[:, None] + jnp.arange(MMAX, dtype=float_type)[None, :]
        geopot = mean_geopot[:, None, None]
        new_v, new_d, new_h = implicit(spectral[:, 0], spectral[:, 1], spectral[:, 2], degree, geopot)
        updated = jnp.stack([new_v, new_d, new_h], axis=1)
        return jnp.einsum('mkj,cflmk->cfljm', legendre, updated, precision=lax.Precision.HIGHEST)
    synthesis = lax.map(solve_block, (jnp.arange(block_count, dtype=jnp.int32), wave_blocks))
    synthesis = jnp.moveaxis(synthesis, 0, 4).reshape(2, 3, LEV, NLAT, MMAX)
    complex_coeffs = lax.complex(synthesis[0], synthesis[1]) * NLON
    complex_coeffs = jnp.pad(complex_coeffs, ((0, 0), (0, 0), (0, 0), (0, NLON // 2 + 1 - MMAX)))
    result = jnp.fft.irfft(complex_coeffs, n=NLON, axis=-1).astype(float_type)
    return (result[0], result[1], result[2])
```

```python
import functools

import jax
import jax.numpy as jnp
import ml_dtypes
import numpy as np
from jax import lax
from jax.experimental import pallas as pl
from jax.experimental.pallas import tpu as pltpu
from jax.sharding import PartitionSpec as P

NLON = 2560
NLAT = 1280
MMAX = 1280
HALF = NLAT // 2

cap_sine = 0.5
filter_width = 64.0
diffusion = 4.0

PACK = 8
GROUP = 8
STEPS = 32
ROWS = GROUP * STEPS
LANES = 256
USED = 192
CHECK = 8
BIG = 2.0**16
DOWN = 2.0**-64


def plan(n_dev):
    waves_dev = MMAX // n_dev
    if waves_dev % GROUP == 0:
        blocks = np.arange(MMAX).reshape(waves_dev // GROUP, n_dev, GROUP)
        blocks[1::2] = blocks[1::2, ::-1].copy()
        return np.transpose(blocks, (1, 0, 2)).reshape(n_dev, waves_dev)
    return np.arange(MMAX).reshape(n_dev, waves_dev)


def first_waves(n_dev, device, group):
    waves_dev = MMAX // n_dev
    if waves_dev % GROUP == 0:
        forth = group * n_dev + device
        back = (group + 1) * n_dev - 1 - device
        return GROUP * jnp.where(group % 2 == 0, forth, back)
    return device * waves_dev + GROUP * group


def fourier_table(n_dev):
    waves = plan(n_dev)
    waves_dev = waves.shape[1]
    groups = -(-waves_dev // GROUP)
    phase = (np.arange(NLON)[:, None] * waves.reshape(-1)[None, :]) % NLON
    angle = 2.0 * np.pi / NLON * np.arange(NLON)
    parts = np.stack([np.cos(angle)[phase], -np.sin(angle)[phase]], axis=1)
    parts = parts.reshape(NLON, 2, n_dev, waves_dev)
    parts = np.pad(parts, ((0, 0), (0, 0), (0, 0), (0, groups * GROUP - waves_dev)))
    parts = parts.reshape(NLON, 2, n_dev, groups, GROUP).transpose(0, 2, 3, 1, 4)
    parts = parts.reshape(NLON, n_dev * groups * 16)
    top = parts.astype(ml_dtypes.bfloat16)
    rest = (parts - top.astype(np.float64)).astype(ml_dtypes.bfloat16)
    return top, rest


def latitudes(row_index):
    colatitude = (4.0 * row_index + 3.0) * jnp.pi / (4.0 * NLAT + 2.0)
    shortfall = 1.0 / (8.0 * NLAT * NLAT) - 1.0 / (8.0 * NLAT * NLAT * NLAT)
    one_minus = shortfall + 2.0 * (1.0 - shortfall) * jnp.sin(0.5 * colatitude) ** 2
    one_plus = shortfall + 2.0 * (1.0 - shortfall) * jnp.cos(0.5 * colatitude) ** 2
    return (0.5 * (one_plus - one_minus), jnp.sqrt(one_minus * one_plus))


def sector_logs():
    sector_order = jnp.arange(1, MMAX, dtype=jnp.float32)
    log_terms = jnp.log2((2.0 * sector_order + 1.0) / (2.0 * sector_order))
    return jnp.concatenate([jnp.zeros((1,), jnp.float32), jnp.cumsum(log_terms)])


def split(value):
    top = value.astype(jnp.bfloat16)
    rest = (value - top.astype(jnp.float32)).astype(jnp.bfloat16)
    return top, rest


def split_outside(value):
    rounded = lax.reduce_precision(value, exponent_bits=8, mantissa_bits=7)
    return rounded.astype(jnp.bfloat16), (value - rounded).astype(jnp.bfloat16)


def matmul(left, right):
    return lax.dot_general(
        left, right, (((1,), (0,)), ((), ())), preferred_element_type=jnp.float32
    )


def legendre_kernel(
    n_dev, levels, geopot_ref, cosine_ref, lead_ref, expo_ref, coef_ref, filter_ref, in_ref,
    out_ref, table_a, table_b, field_top, field_rest, total, prev_ref, cur_ref, exp_ref, turned,
    ready,
):
    device = lax.axis_index("lat") * lax.axis_size("lon") + lax.axis_index("lon")
    first = first_waves(n_dev, device, pl.program_id(0))
    pairs = lax.div(MMAX - first + 2 * STEPS - 1, 2 * STEPS)

    sub_rows = NLAT // n_dev
    packs = n_dev // PACK
    lane = lax.broadcasted_iota(jnp.int32, (sub_rows, 128), 1)
    sign = jnp.where((lane // 32) % 2 == 0, 1.0, -1.0)

    def at(row_block):
        return pl.ds(row_block * sub_rows, sub_rows)

    for pack in range(packs):
        block = in_ref[pack * PACK : (pack + 1) * PACK, 0].reshape(PACK * 16, LANES)
        turned[pack] = jnp.transpose(block, (1, 0))
    for north in range(n_dev // 2):
        south = n_dev - 1 - north
        weight = filter_ref[0, at(north), :]

        def gather(source, which, place):
            rows = pl.ds(which * sub_rows, sub_rows)
            value = turned[source // PACK, rows, :]
            return pltpu.roll(value, (place - (source % PACK) * 16) % 128, 1)

        halves = [jnp.zeros((sub_rows, 128), jnp.float32)] * 2
        for which in range(3 * levels):
            kind, level = which // levels, which % levels
            for parity in range(2):
                place = (kind % 2) * 64 + parity * 32 + level * 16
                value = gather(north, which, place) + sign * gather(south, which, place)
                here = (lane >= place) & (lane < place + 16)
                halves[kind // 2] = jnp.where(here, value, halves[kind // 2])
        for half in range(2):
            top, rest = split(halves[half] * weight)
            field_top[at(north), half * 128 : (half + 1) * 128] = top
            field_top[pl.ds(HALF + north * sub_rows, sub_rows), half * 128 : (half + 1) * 128] = top
            field_rest[at(north), half * 128 : (half + 1) * 128] = rest
    total[...] = jnp.zeros_like(total)

    lane = lax.broadcasted_iota(jnp.int32, (GROUP, 128), 1)
    sub = lax.broadcasted_iota(jnp.int32, (GROUP, 128), 0)
    same = lane % GROUP == sub
    even = jnp.where(same & ((lane // 32) % 2 == 0), 1.0, 0.0)
    odd = jnp.where(same & ((lane // 32) % 2 == 1), 1.0, 0.0)
    second_level = (lane // 16) % 2 == 1
    geopot = jnp.where(second_level, geopot_ref[1], geopot_ref[0])
    is_div = lane < 64
    cosine = jnp.broadcast_to(cosine_ref[...], (GROUP, HALF))

    def generate(chunk, table_ref):
        coefs = coef_ref[0, chunk]
        previous, current, exponent = prev_ref[...], cur_ref[...], exp_ref[...]
        values = []
        for step in range(STEPS):
            if step % CHECK == 0:
                large = jnp.abs(current) > BIG
                factor = jnp.where(large, DOWN, 1.0)
                current = current * factor
                previous = previous * factor
                exponent = exponent + jnp.where(large, 1.0, 0.0)
                scale = jnp.where(exponent >= 0.0, 1.0, jnp.where(exponent >= -1.0, DOWN, 0.0))
            forward = coefs[:, step : step + 1]
            backward = coefs[:, STEPS + step : STEPS + step + 1]
            previous, current = current, forward * (cosine * current) - backward * previous
            values.append(current * scale)
            if len(values) == 2:
                top, rest = split(jnp.concatenate(values, axis=0))
                place = pl.ds((step - 1) * GROUP, 2 * GROUP)
                table_ref[place, :HALF] = top
                table_ref[place, HALF:] = rest
                values = []
        prev_ref[...], cur_ref[...], exp_ref[...] = previous, current, exponent

    def transform(chunk, table_ref):
        spectral = matmul(table_ref[...], field_top[...])
        spectral += matmul(table_ref[:, :HALF], field_rest[...])
        coefs = coef_ref[0, chunk]

        def coef(which, step):
            place = which * STEPS + step
            return jnp.broadcast_to(coefs[:, place : place + 1], (GROUP, 128))

        left, right = [], []
        for step in range(STEPS):
            rows = slice(step * GROUP, (step + 1) * GROUP)
            first_half, height = spectral[rows, :128], spectral[rows, 128:]
            coupling = coef(2, step)
            damping = coef(3, step) * (even if step % 2 == 0 else odd)
            inverse = jnp.where(second_level, coef(5, step), coef(4, step))
            div_new = (first_half + coupling * height) * inverse
            height_new = height - geopot * coupling * div_new
            left.append(jnp.where(is_div, div_new, first_half) * damping)
            right.append(height_new * damping)
        updated = jnp.concatenate(
            [jnp.concatenate(left, axis=0), jnp.concatenate(right, axis=0)], axis=1
        )
        flipped = jnp.transpose(updated, (1, 0))[:USED]
        new_top, new_rest = split(flipped)
        both = matmul(jnp.concatenate([new_top, new_rest], axis=0), table_ref[:, :HALF])
        total[...] += both[:USED] + both[USED:] + matmul(new_top, table_ref[:, HALF:])

    prev_ref[...] = lead_ref[0]
    cur_ref[...] = jnp.zeros_like(cur_ref)
    exp_ref[...] = expo_ref[0]
    generate(0, table_a)

    def body(pair, carry):
        generate(2 * pair + 1, table_b)
        transform(2 * pair, table_a)
        generate(2 * pair + 2, table_a)
        transform(2 * pair + 1, table_b)
        return carry

    lax.fori_loop(0, pairs, body, 0)

    summed = jnp.transpose(total[...], (1, 0))
    ready[:, :USED] = summed
    lane = lax.broadcasted_iota(jnp.int32, (sub_rows, 128), 1)
    for pack in range(packs):
        for which in range(3 * levels):
            kind, level = which // levels, which % levels
            value = jnp.zeros((sub_rows, 128), jnp.float32)
            for slot in range(PACK):
                target = pack * PACK + slot
                north = target < n_dev // 2
                rows = at(target if north else n_dev - 1 - target)
                source = ready[rows, (kind // 2) * 128 : (kind // 2 + 1) * 128]
                place = (kind % 2) * 64 + level * 16
                even_part = pltpu.roll(source, (slot * 16 - place) % 128, 1)
                odd_part = pltpu.roll(source, (slot * 16 - place - 32) % 128, 1)
                joined = even_part + odd_part if north else even_part - odd_part
                here = (lane >= slot * 16) & (lane < slot * 16 + 16)
                value = jnp.where(here, joined, value)
            turned[pack, pl.ds(which * sub_rows, sub_rows), :] = value
        out_ref[pack * PACK : (pack + 1) * PACK, 0] = jnp.transpose(turned[pack], (1, 0)).reshape(
            PACK, 16, LANES
        )


def legendre_step(n_dev, levels, mean_geopot, cosine, lead, expo, coefs, filtering, columns):
    groups = columns.shape[1]
    chunks = coefs.shape[1]
    return pl.pallas_call(
        functools.partial(legendre_kernel, n_dev, levels),
        grid=(groups,),
        out_shape=jax.ShapeDtypeStruct(columns.shape, jnp.float32),
        in_specs=[
            pl.BlockSpec(memory_space=pltpu.SMEM),
            pl.BlockSpec((1, HALF), lambda i: (0, 0)),
            pl.BlockSpec((1, GROUP, HALF), lambda i: (i, 0, 0)),
            pl.BlockSpec((1, GROUP, HALF), lambda i: (i, 0, 0)),
            pl.BlockSpec((1, chunks, GROUP, 6 * STEPS), lambda i: (i, 0, 0, 0)),
            pl.BlockSpec((1, HALF, 128), lambda i: (i, 0, 0)),
            pl.BlockSpec((n_dev, 1, 16, LANES), lambda i: (0, i, 0, 0)),
        ],
        out_specs=pl.BlockSpec((n_dev, 1, 16, LANES), lambda i: (0, i, 0, 0)),
        scratch_shapes=[pltpu.VMEM((ROWS, 2 * HALF), jnp.bfloat16)] * 2
        + [pltpu.VMEM((2 * HALF, LANES), jnp.bfloat16), pltpu.VMEM((HALF, LANES), jnp.bfloat16)]
        + [pltpu.VMEM((USED, HALF), jnp.float32)]
        + [pltpu.VMEM((GROUP, HALF), jnp.float32)] * 3
        + [pltpu.VMEM((n_dev // PACK, LANES, PACK * 16), jnp.float32)]
        + [pltpu.VMEM((HALF, LANES), jnp.float32)],
        compiler_params=pltpu.CompilerParams(vmem_limit_bytes=40 * 2**20),
    )(mean_geopot, cosine[None, :], lead, expo, coefs, filtering, columns)


def coefficients(waves, mean_geopot):
    groups = waves.shape[0]
    chunks = MMAX // STEPS + 2
    wave = waves[:, None, :, None]
    excess = jnp.arange(chunks * STEPS, dtype=jnp.float32).reshape(1, chunks, 1, STEPS)
    degree = wave + excess
    growth = jnp.sqrt(
        (4.0 * degree * degree - 1.0) / jnp.maximum(excess * (2.0 * wave + excess), 1.0)
    )
    backward = jnp.sqrt(
        jnp.maximum((excess - 1.0) * (2.0 * wave + excess - 1.0), 0.0)
        / jnp.maximum(4.0 * (degree - 1.0) ** 2 - 1.0, 1.0)
    )
    start = excess == 0.0
    lap_ratio = degree * (degree + 1.0) / (MMAX * MMAX)
    damping = jnp.where(degree < MMAX, 1.0 / (1.0 + diffusion * lap_ratio * lap_ratio), 0.0)
    damping = damping * jnp.where(wave == 0.0, 1.0, 2.0)
    kinds = [
        jnp.where(start, 0.0, growth),
        jnp.where(start, -1.0, growth * backward),
        jnp.sqrt(lap_ratio),
        damping,
        1.0 / (1.0 + mean_geopot[0] * lap_ratio),
        1.0 / (1.0 + mean_geopot[1] * lap_ratio),
    ]
    shape = (groups, chunks, GROUP, STEPS)
    return jnp.concatenate([jnp.broadcast_to(kind, shape) for kind in kinds], axis=-1)


def shards(vorticity, divergence, height, mean_geopot):
    n_lat = lax.axis_size("lat")
    n_lon = lax.axis_size("lon")
    n_dev = n_lat * n_lon
    device = lax.axis_index("lat") * n_lon + lax.axis_index("lon")
    levels = vorticity.shape[0]
    sub_rows = vorticity.shape[1] // n_lon
    waves_dev = MMAX // n_dev
    groups = -(-waves_dev // GROUP)

    kinds = 3 * levels
    rows = kinds * sub_rows
    southern = lax.axis_index("lat") >= n_lat // 2

    def mirror(value):
        return jnp.where(southern, jnp.flip(value, 1), value)

    def exchange(value, axes):
        return lax.all_to_all(value, axes, split_axis=0, concat_axis=0, tiled=True)

    stacked = jnp.stack([divergence, vorticity, height])
    stacked = stacked.reshape(kinds, n_lon, sub_rows, NLON // n_lon)
    sectors = exchange(jnp.moveaxis(stacked, 1, 0), "lon")
    sectors = mirror(jnp.transpose(sectors, (1, 2, 0, 3)).reshape(kinds, sub_rows, NLON))
    sectors = jnp.pad(sectors.reshape(rows, NLON), ((0, LANES - rows), (0, 0)))
    table_top, table_rest = (jnp.asarray(part) for part in fourier_table(n_dev))
    top, rest = split_outside(sectors)
    across = functools.partial(
        lax.dot_general,
        dimension_numbers=(((0,), (1,)), ((), ())),
        preferred_element_type=jnp.float32,
    )
    spectrum = across(table_top, top) + across(table_top, rest) + across(table_rest, top)
    columns = exchange(spectrum.reshape(n_dev, groups, 16, LANES), ("lat", "lon"))

    first = first_waves(n_dev, device, jnp.arange(groups))
    waves = (first[:, None] + jnp.arange(GROUP)[None, :]).astype(jnp.float32)
    cosine, sine_theta = latitudes(jnp.arange(HALF, dtype=jnp.float32))
    weight = jnp.pi * sine_theta / (NLAT + 0.5) / NLON
    lane_waves = jnp.tile(waves, (1, 16))[:, None, :]
    excess = (
        jnp.maximum(lane_waves - MMAX * sine_theta[:, None] / cap_sine, 0.0) / filter_width
    )
    filtering = weight[:, None] * jnp.exp(-0.5 * excess * excess)

    cumlog = jnp.take(sector_logs(), jnp.minimum(waves.astype(jnp.int32), MMAX - 1))
    log_start = -0.5 + 0.5 * cumlog[:, :, None] + waves[:, :, None] * jnp.log2(sine_theta)
    exponent = jnp.floor(log_start)
    leading = jnp.exp2(log_start - exponent)
    turns = jnp.floor((exponent + 48.0) / 64.0)
    lead = leading * jnp.exp2(exponent - 64.0 * turns)

    synthesis = legendre_step(
        n_dev, levels, mean_geopot, cosine, lead, turns, coefficients(waves, mean_geopot),
        filtering, columns,
    )
    gathered = exchange(synthesis, ("lat", "lon")).reshape(-1, LANES)
    top, rest = split_outside(gathered)
    back = functools.partial(
        lax.dot_general,
        dimension_numbers=(((0,), (1,)), ((), ())),
        preferred_element_type=jnp.float32,
    )
    result = back(top, table_top) + back(rest, table_top) + back(top, table_rest)
    result = mirror(result[:rows].reshape(kinds, sub_rows, NLON))
    result = result.reshape(kinds, sub_rows, n_lon, NLON // n_lon)
    pieces = exchange(jnp.transpose(result, (2, 0, 1, 3)), "lon")
    pieces = jnp.moveaxis(pieces, 0, 1).reshape(3, levels, n_lon * sub_rows, NLON // n_lon)
    return (pieces[1], pieces[0], pieces[2])


def solution(mesh):
    placed = P(None, "lat", "lon")
    return jax.shard_map(
        shards,
        mesh=mesh,
        in_specs=(placed, placed, placed, P()),
        out_specs=(placed, placed, placed),
        check_vma=False,
    )
```
